32 devices in a mesh: freq: 2 (over y), cell: 4 (over z), sub: 4 (over x, core).
Axes of the slice: x: 2, y: 2, z: 4, core: 2. Of those that a mesh axis runs over, the one named last changes fastest.
Arguments:
- direction: float32 [4, 240, 2048], P('freq', 'sub', 'cell'), parts along dimension 0, may hold values from -6 to 6
- neighbours: int32 [12, 2048], P(None, 'cell'), may hold values from 0 to 2047, as said below
- spacing: float32 [12, 2048], P(None, 'cell'), may hold values from 1 to 3
- scatterer: int32 [2048, 1], P('cell'), may hold values from 0 to 15; in each aligned block of 512 rows (0 to 511, 512 to 1023, ...) at most 128 rows name the same one
- box_index: int32 [2048], P('cell'), may hold values from 0 to 63, as said below
- translation: float32 [16, 240, 480], P(None, 'sub', 'freq'), parts along dimension 2, may hold values from -0.046875 to 0.046875
- response: float32 [16, 240, 480], P('cell', 'sub', 'freq'), parts along dimension 2, may hold values from -0.375 to 0.375
- coarse_map: float32 [240, 480], P('sub', 'freq'), parts along dimension 1, may hold values from -0.015625 to 0.015625
Outputs:
- product: float32 [4, 240, 2048], P('freq', 'sub', 'cell'), parts along dimension 0
The draws below stay inside these ranges and needn't reach their ends.
There are 2 independent parts, one for each index of `freq`. The reference program is written for one: setup_inputs(seed, part) draws one part's arguments, and reference() takes and returns one part's arrays. A program takes and returns all parts, laid end to end along the dimension named above; an argument that names none is the same for every part. Nothing has to cross between parts.
Inputs may be any that keep to these rules, and one draw needn't show every extreme that they name: neighbours[n, i] differs from i by 1 to 128; neighbours[0, i] differs from i by exactly 128. `box_index`: non-decreasing; the j-th block of 512 meta-atoms holds exactly the boxes j * 16 to (j + 1) * 16 - 1, each with one meta-atom or more. `scatterer`: among the meta-atoms of one index of cell no type occurs more than 128 times.
All inputs are finite; a program needn't handle non-finite values.
Results may differ from the reference program's by a relative error of at most 0.000052.
Values sent between devices are 32-bit elements; how exact they have to be, the bound alone decides.
A program may use at most 64 MiB of HBM per device.

```python
import math
import jax
import jax.numpy as jnp
import numpy as np
from jax import lax

COEF = 120
NRHS = 2
ATOM_DEV = 512
NB = 12
QTERMS = 16
BOX_DEV = 16
WIN = 128
ATOMS = 2048
TYPES = 16
BOXES = 64
MOST = 128


def draw_neighbours(key, part):
    key = jax.random.fold_in(key, 11)
    first_key, second_key = jax.random.split(key)
    reach = jax.random.randint(first_key, (NB, ATOMS), 1, WIN + 1)
    reach = reach.at[0].set(WIN)
    polarity = 2 * jax.random.randint(second_key, (NB, ATOMS), 0, 2) - 1
    offset = polarity * reach
    anchor = jnp.arange(ATOMS, dtype=jnp.int32)[None, :]
    guess = anchor + offset
    inside = (guess >= 0) & (guess < ATOMS)
    return jnp.where(inside, guess, anchor - offset).astype(jnp.int32)


def draw_box_index(key, part):
    key = jax.random.fold_in(key, 23)
    blocks = ATOMS // ATOM_DEV
    block_keys = jax.random.split(key, blocks)

    def one_block(block_key):
        order = jax.random.permutation(block_key, ATOM_DEV - 1) + 1
        cuts = jnp.sort(order[:BOX_DEV - 1])
        places = jnp.arange(ATOM_DEV, dtype=jnp.int32)
        return jnp.sum((places[:, None] >= cuts[None, :]).astype(jnp.int32), axis=1).astype(jnp.int32)
    within = jax.vmap(one_block)(block_keys)
    firsts = (jnp.arange(blocks, dtype=jnp.int32) * BOX_DEV)[:, None]
    return (within + firsts).reshape(ATOMS).astype(jnp.int32)


def block_scale(stream_key, dims, shards, least, largest):
    loudness = 1.0
    for dim, blocks in shards:
        heights = jax.random.uniform(jax.random.fold_in(jax.random.fold_in(stream_key, 6), dim), (blocks,), jnp.float32, least / len(shards), largest / len(shards))
        loudness = loudness * jnp.repeat(jnp.exp(heights), dims[dim] // blocks).reshape((-1,) + (1,) * (len(dims) - 1 - dim))
    return loudness


def deal_out(stream_key, own, number, rows, count, top, bound, skew):
    ranking = jax.random.permutation(stream_key, count)
    crowded, common = portions_of(count, rows * top, bound, skew, True), portions_of(count, rows * top, bound, skew, False)
    places = jnp.arange(count)

    def named(tallies, turn):
        used = int((tallies > 0).sum())
        fixed = max(1, used // 4)
        passed = fixed + (places - fixed + turn * (used - fixed)) % max(1, count - fixed)
        return jnp.zeros((count,), jnp.int32).at[ranking[jnp.where(places < fixed, places, passed)]].set(jnp.asarray(tallies, jnp.int32))

    tallies = jnp.where(number % 4 == 0, named(crowded, number // 4), named(common, number - number // 4 - 1))
    mixed = jax.random.permutation(jax.random.fold_in(own, 3), count)
    source_of, taker = mixed[0:count // 2 * 2:2], mixed[1:count // 2 * 2:2]
    slack = jnp.minimum(tallies[source_of] - 1, bound - tallies[taker]) // 2
    slack = jnp.where((source_of == ranking[0]) | (taker == ranking[0]) | (tallies[taker] == 0), 0, jnp.maximum(slack, 0))
    passed = jax.random.randint(jax.random.fold_in(own, 4), (count // 2,), 0, 1 << 20) % (slack + 1)
    tallies = tallies.at[source_of].add(-passed).at[taker].add(passed)
    items = jnp.searchsorted(jnp.cumsum(tallies), jnp.arange(rows * top), side="right").astype(jnp.int32)
    grid = items.reshape(top, rows).T
    grid = grid[jax.random.permutation(jax.random.fold_in(own, 1), rows)]
    turn = jax.random.randint(jax.random.fold_in(own, 2), (rows, 1), 0, top)
    return jnp.take_along_axis(grid, (jnp.arange(top)[None, :] + turn) % top, axis=1)


def portions_of(amount, total, bound, slope, full):
    portions = [(1 << 20) // math.isqrt(grade ** slope) + 1 for grade in range(1, amount + 1)]
    largest = bound if full else min(bound, max(-(-total // amount), total * portions[0] // sum(portions)))
    least = 1 if total - largest >= amount - 1 else 0
    given, rest = [largest] + [least] * (amount - 1), total - largest - least * (amount - 1)
    while rest > 0:
        candidates = [i for i in range(1, amount) if given[i] < largest] or [i for i in range(1, amount) if given[i] < bound]
        whole, left = sum([portions[i] for i in candidates]), rest
        for i in candidates:
            extra = min(bound - given[i], max(1, left * portions[i] // whole), rest)
            given[i] = given[i] + extra
            rest = rest - extra
    return np.array(given)


def centred(own_key, extent, width, limit, cuts=(), held_as=jnp.bfloat16):
    result = jax.random.normal(own_key, extent, jnp.float32) * width
    if len(cuts) > 0:
        result = block_scale(own_key, extent, cuts, -0.22, 0.18) * result
    return jnp.clip(result, min=-limit, max=limit).astype(held_as)


def setup_inputs(seed: int = 0, part: int = 0) -> dict:
    arg_keys = jax.random.split(jax.random.key(seed), 9)
    part_keys = jax.random.split(jax.random.fold_in(arg_keys[8], part), 9)
    direction = centred(part_keys[0], (NRHS, 2 * COEF, ATOMS), 1.0, 6.0, ((1, 4), (2, 4)), jnp.float32)
    neighbours = draw_neighbours(jax.random.fold_in(arg_keys[8], 71), part)
    spacing = jnp.clip(1.0 + 2.0 * jax.random.uniform(arg_keys[2], (NB, ATOMS), jnp.float32) ** block_scale(arg_keys[2], (NB, ATOMS), ((1, 4),), -0.2, 0.2), 1.0, 3.0)
    scatterer_keys = jax.random.split(jax.random.fold_in(arg_keys[3], 1), ATOMS // ATOM_DEV)
    scatterer_turns = jax.random.permutation(jax.random.fold_in(arg_keys[3], 3), ATOMS // ATOM_DEV)
    scatterer = jax.vmap(lambda own, number: deal_out(jax.random.fold_in(arg_keys[3], 2), own, number, ATOM_DEV, TYPES, 1, MOST, 2))(scatterer_keys, scatterer_turns).reshape((ATOMS, 1))
    box_index = draw_box_index(jax.random.fold_in(arg_keys[8], 71), part)
    translation = centred(part_keys[5], (QTERMS, 2 * COEF, 2 * COEF), (2 * COEF * NB * QTERMS // 3) ** -0.5, 0.046875, ((1, 4),), jnp.float32)
    response = centred(part_keys[6], (TYPES, 2 * COEF, 2 * COEF), (2 * COEF) ** -0.5, 0.375, ((0, 4), (1, 4)), jnp.float32)
    coarse_map = centred(part_keys[7], (2 * COEF, 2 * COEF), (2 * COEF * ATOM_DEV) ** -0.5, 0.015625, ((0, 4),), jnp.float32)
    return dict(direction=direction, neighbours=neighbours, spacing=spacing, scatterer=scatterer, box_index=box_index, translation=translation, response=response, coarse_map=coarse_map)


def coupling(distance):
    orders = jnp.arange(QTERMS).astype(jnp.float32)
    return jnp.cos(0.9 * orders[None, :, None] * distance[:, None, :]) / distance[:, None, :]

def reference(direction, neighbours, spacing, scatterer, box_index, translation, response, coarse_map):
    highest = lax.Precision.HIGHEST
    nrhs_count = direction.shape[0]
    row_count = direction.shape[1]
    starts = jnp.arange(ATOMS // ATOM_DEV).astype(jnp.int32) * ATOM_DEV

    def near_block(start):
        chosen = lax.dynamic_slice_in_dim(neighbours, start, ATOM_DEV, 1)
        distance = lax.dynamic_slice_in_dim(spacing, start, ATOM_DEV, 1)
        weights = coupling(distance)
        picked = direction[:, :, chosen]
        mixed = jnp.einsum('nqa,kcna->qkca', weights, picked, precision=highest)
        return jnp.einsum('qrc,qkca->kra', translation, mixed, precision=highest)
    near_parts = lax.map(near_block, starts)
    near = jnp.moveaxis(near_parts, 0, 2).reshape(nrhs_count, row_count, ATOMS)
    members = (box_index[:, None] == jnp.arange(BOXES).astype(jnp.int32)[None, :]).astype(jnp.float32)
    box_sums = jnp.einsum('kca,ab->kcb', direction, members, precision=highest)
    offsets = (jnp.arange(BOXES)[:, None] - jnp.arange(BOXES)[None, :]).astype(jnp.float32)
    kernel = jnp.where(offsets == 0.0, jnp.float32(0.0), jnp.cos(1.3 * offsets) / jnp.sqrt(jnp.maximum(jnp.abs(offsets), 1.0)))
    local = jnp.einsum('kcb,bd->kcd', box_sums, kernel, precision=highest)
    far_box = jnp.einsum('rc,kcd->krd', coarse_map, local, precision=highest)
    far = far_box[:, :, box_index]
    incident = near + far
    kinds_all = scatterer[:, 0]

    def apply_block(start):
        kinds = lax.dynamic_slice_in_dim(kinds_all, start, ATOM_DEV, 0)
        matrices = response[kinds]
        field = lax.dynamic_slice_in_dim(incident, start, ATOM_DEV, 2)
        return jnp.einsum('arc,kca->kra', matrices, field, precision=highest)
    scattered_parts = lax.map(apply_block, starts)
    scattered = jnp.moveaxis(scattered_parts, 0, 2).reshape(nrhs_count, row_count, ATOMS)
    return direction - scattered
```

```python
import functools

import jax
import jax.numpy as jnp
from jax import lax
from jax.experimental import pallas as pl
from jax.experimental.pallas import tpu as pltpu
from jax.sharding import PartitionSpec as P

BOX_DEV = 16
WIN = 128
BLK = 128
MESH = pl.DeviceIdType.MESH
F32 = jnp.float32
BF16 = jnp.bfloat16
HIGHEST = lax.Precision.HIGHEST


def split(x):
    high = x.astype(BF16)
    return high, (x - high.astype(F32)).astype(BF16)


def dot3(ah, al, bh, bl):
    dot = functools.partial(jnp.dot, preferred_element_type=F32)
    return dot(ah, bh) + (dot(ah, bl) + dot(al, bh))


def kernel(
    cells, subs,
    dir_ref, nbr_ref, spc_ref, kind_ref, box_ref, t_ref, r_ref, cm_ref, out_ref,
    ext, gown, gall, rsend, rall, inc, wts, nls, w2, y2, tpad, dfull, dh, dl, rh, rl, ffull,
    dir_send, dir_recv, halo_send, halo_recv, r_send, r_recv, g_send, g_recv, inc_send, inc_recv,
):
    nrhs, rows, atoms = dir_ref.shape
    nb, terms = nbr_ref.shape[0], t_ref.shape[0]
    types, full = r_ref.shape[0], r_ref.shape[2]
    blocks = atoms // BLK
    span = BLK + 2 * WIN
    pad = 64
    cell, sub = lax.axis_index("cell"), lax.axis_index("sub")
    has_left, has_right = cell > 0, cell < cells - 1

    def copy(src, dst, send, recv, to_cell, to_sub):
        return pltpu.make_async_remote_copy(
            src_ref=src, dst_ref=dst, send_sem=send, recv_sem=recv,
            device_id={"cell": to_cell, "sub": to_sub}, device_id_type=MESH,
        )

    def each_far_cell(body):
        def step(other, carry):
            @pl.when(other != cell)
            def _():
                body(other)
            return carry
        lax.fori_loop(0, cells, step, 0)

    barrier = pltpu.get_barrier_semaphore()

    def greet(to_cell, to_sub):
        pl.semaphore_signal(
            barrier, inc=1, device_id={"cell": to_cell, "sub": to_sub}, device_id_type=MESH
        )

    for d in range(1, subs):
        greet(cell, lax.rem(sub + d, subs))
    for present, other in ((has_left, cell - 1), (has_right, cell + 1)):
        @pl.when(present)
        def _():
            for d in range(1, subs):
                greet(other, lax.rem(sub + d, subs))
    each_far_cell(lambda other: greet(other, sub))
    sides = has_left.astype(jnp.int32) + has_right.astype(jnp.int32)
    pl.semaphore_wait(barrier, (subs - 1) * (1 + sides) + cells - 1)

    def dir_copy(d):
        return copy(
            dir_ref, ext.at[sub, :, :, pl.ds(WIN, atoms)], dir_send.at[d], dir_recv.at[sub],
            cell, lax.rem(sub + d, subs),
        )

    def halo_copy(side, d):
        start = atoms - WIN if side == 0 else 0
        place = 0 if side == 0 else WIN + atoms
        other = cell + 1 if side == 0 else cell - 1
        return copy(
            dir_ref.at[:, :, pl.ds(start, WIN)], ext.at[sub, :, :, pl.ds(place, WIN)],
            halo_send.at[side, d], halo_recv.at[side, sub], other, lax.rem(sub + d, subs),
        )

    def r_copy(other):
        return copy(rsend, rall.at[cell], r_send.at[other], r_recv.at[cell], other, sub)

    def g_copy(other):
        return copy(gown, gall.at[cell], g_send.at[other], g_recv.at[cell], other, sub)

    def inc_copy(b, d):
        return copy(
            inc.at[sub, b], inc.at[sub, b], inc_send.at[b, d], inc_recv.at[b, sub],
            cell, lax.rem(sub + d, subs),
        )

    for d in range(1, subs):
        dir_copy(d).start()
    for side, present in ((0, has_right), (1, has_left)):
        @pl.when(present)
        def _():
            for d in range(subs):
                halo_copy(side, d).start()
    for side, present in ((0, has_left), (1, has_right)):
        @pl.when(jnp.logical_not(present))
        def _():
            place = 0 if side == 0 else WIN + atoms
            ext[:, :, :, pl.ds(place, WIN)] = jnp.zeros((subs, nrhs, rows, WIN), F32)
    ext[sub, :, :, pl.ds(WIN, atoms)] = dir_ref[...]

    rsend[...] = jnp.zeros_like(rsend)
    for t in range(types):
        rsend[t * pad:t * pad + rows, :] = r_ref[t]
    each_far_cell(lambda other: r_copy(other).start())
    rall[cell] = rsend[...]

    orders = lax.broadcasted_iota(jnp.int32, (terms, 1), 0).astype(F32)
    wide = nbr_ref[...] - (cell * atoms - WIN)
    near_rows = [wide[n:n + 1] for n in range(nb)]
    plain = []
    for n in range(nb):
        s = spc_ref[n:n + 1, :]
        plain.append(jnp.cos(0.9 * orders * s) / s)
    dead = [None] * nb
    for n in range(nb):
        total = plain[n]
        for m in range(n + 1, nb):
            same = near_rows[n] == near_rows[m]
            total = total + jnp.where(same, plain[m], 0.0)
            flag = same.astype(jnp.int32)
            dead[m] = flag if dead[m] is None else dead[m] | flag
        wts[n] = total
        row = near_rows[n]
        if dead[n] is not None:
            row = jnp.where(dead[n] > 0, -1, row)
        nls[n:n + 1, :] = row

    chunk, group = 32, 8
    for b in range(blocks):
        lanes = slice(b * BLK, (b + 1) * BLK)

        def spread(step, carry):
            base = lax.broadcasted_iota(jnp.int32, (chunk, BLK), 0) + (b * BLK + step * chunk)
            for q0 in range(0, terms, group):
                acc = [jnp.zeros((chunk, BLK), F32)] * group
                for n in range(nb):
                    hit = nls[n:n + 1, lanes] == base
                    for q in range(group):
                        acc[q] = jnp.where(hit, wts[n, q0 + q:q0 + q + 1, lanes], acc[q])
                for q in range(group):
                    high, low = split(acc[q])
                    place = pl.ds(pl.multiple_of((q0 + q) * span + step * chunk, chunk), chunk)
                    w2[b, place, 0:BLK] = high
                    w2[b, place, BLK:2 * BLK] = low
            return carry

        lax.fori_loop(0, span // chunk, spread, 0)

    tpad[...] = jnp.zeros_like(tpad)
    for q in range(terms):
        tpad[q * pad:q * pad + rows, :] = t_ref[q]

    for d in range(1, subs):
        other = lax.rem(sub + d, subs)
        piece = ext.at[other, :, :, pl.ds(WIN, atoms)]
        copy(piece, piece, dir_send.at[d], dir_recv.at[other], cell, other).wait_recv()
    for s in range(subs):
        for k in range(nrhs):
            dfull[k, s * rows:(s + 1) * rows, WIN:WIN + atoms] = ext[s, k, :, WIN:WIN + atoms]

    first_box = cell * BOX_DEV
    box_ids = lax.broadcasted_iota(jnp.int32, (BOX_DEV, 1), 0) + first_box
    member = (box_ref[...] == box_ids).astype(F32)
    member_h = member.astype(BF16)
    gown[...] = jnp.zeros_like(gown)
    nt = (((1,), (1,)), ((), ()))
    for k in range(nrhs):
        ch, cl = split(dfull[k, :, WIN:WIN + atoms])
        dh[k, :, WIN:WIN + atoms] = ch
        dl[k, :, WIN:WIN + atoms] = cl
        sums = lax.dot_general(ch, member_h, nt, preferred_element_type=F32) + lax.dot_general(
            cl, member_h, nt, preferred_element_type=F32
        )
        gown[k * pad:k * pad + rows, :] = jnp.dot(
            cm_ref[...], sums, precision=HIGHEST, preferred_element_type=F32
        )
    each_far_cell(lambda other: g_copy(other).start())
    gall[cell] = gown[...]

    for side, present in ((0, has_left), (1, has_right)):
        @pl.when(present)
        def _():
            place = 0 if side == 0 else WIN + atoms
            for s in range(subs):
                piece = ext.at[s, :, :, pl.ds(place, WIN)]
                copy(
                    piece, piece, halo_send.at[side, s], halo_recv.at[side, s], cell, s
                ).wait_recv()
    for place in (0, WIN + atoms):
        lanes = slice(place, place + WIN)
        for k in range(nrhs):
            for s in range(subs):
                dfull[k, s * rows:(s + 1) * rows, lanes] = ext[s, k, :, lanes]
            high, low = split(dfull[k, :, lanes])
            dh[k, :, lanes] = high
            dl[k, :, lanes] = low

    per = 4
    for q0 in range(0, terms, per):
        th, tl = split(tpad[q0 * pad:(q0 + per) * pad, :])
        for k in range(nrhs):
            high, low = split(dot3(th, tl, dh[k], dl[k]))
            for q in range(per):
                y2[q0 + q, k * pad:(k + 1) * pad, :] = high[q * pad:(q + 1) * pad]
                y2[q0 + q, (nrhs + k) * pad:(nrhs + k + 1) * pad, :] = low[q * pad:(q + 1) * pad]

    def wait_g(other):
        copy(gown, gall.at[other], g_send.at[other], g_recv.at[other], other, sub).wait_recv()

    each_far_cell(wait_g)
    far_box = jnp.zeros((nrhs * pad, BOX_DEV), F32)
    row_id = lax.broadcasted_iota(jnp.int32, (BOX_DEV, BOX_DEV), 0)
    col_id = lax.broadcasted_iota(jnp.int32, (BOX_DEV, BOX_DEV), 1)
    for c in range(cells):
        offsets = ((row_id + c * BOX_DEV) - (col_id + first_box)).astype(F32)
        green = jnp.where(
            offsets == 0.0, 0.0,
            jnp.cos(1.3 * offsets) / jnp.sqrt(jnp.maximum(jnp.abs(offsets), 1.0)),
        )
        far_box += jnp.dot(gall[c], green, precision=HIGHEST, preferred_element_type=F32)
    fbh, fbl = split(far_box)

    half = nrhs * pad
    for b in range(blocks):
        window = slice(b * BLK, b * BLK + span)
        left = jnp.concatenate([y2[q, :, window] for q in range(terms)], axis=1)
        prod = jnp.dot(left, w2[b], preferred_element_type=F32)
        near = (prod[:half, :BLK] + (prod[:half, BLK:] + prod[half:, :BLK])) + prod[half:, BLK:]
        mb = member_h[:, b * BLK:(b + 1) * BLK]
        far = jnp.dot(fbh, mb, preferred_element_type=F32) + jnp.dot(
            fbl, mb, preferred_element_type=F32
        )
        inc[sub, b] = near + far
        for d in range(1, subs):
            inc_copy(b, d).start()

    def wait_r(other):
        copy(rsend, rall.at[other], r_send.at[other], r_recv.at[other], other, sub).wait_recv()

    each_far_cell(wait_r)

    def split_r(c, carry):
        rh[c], rl[c] = split(rall[c])
        return carry

    lax.fori_loop(0, cells, split_r, 0)

    for b in range(blocks):
        lanes = slice(b * BLK, (b + 1) * BLK)
        for d in range(1, subs):
            other = lax.rem(sub + d, subs)
            piece = inc.at[other, b]
            copy(piece, piece, inc_send.at[b, d], inc_recv.at[b, other], cell, other).wait_recv()
        for s in range(subs):
            for k in range(nrhs):
                ffull[s * rows:(s + 1) * rows, k * BLK:(k + 1) * BLK] = inc[
                    s, b, k * pad:k * pad + rows, :
                ]
        fh, fl = split(ffull[...])
        kinds = kind_ref[:, lanes]
        kinds = jnp.concatenate([kinds] * nrhs, axis=1)

        def apply(c, total):
            prod = dot3(rh[c], rl[c], fh, fl)
            for t in range(types):
                total = jnp.where(kinds == c * types + t, prod[t * pad:(t + 1) * pad], total)
            return total

        total = jnp.zeros((pad, nrhs * BLK), F32)
        if cells <= 4:
            for c in range(cells):
                total = apply(c, total)
        else:
            total = lax.fori_loop(0, cells, apply, total)
        for k in range(nrhs):
            out_ref[k, :, lanes] = dir_ref[k, :, lanes] - total[:rows, k * BLK:(k + 1) * BLK]

    for d in range(1, subs):
        dir_copy(d).wait_send()
        for b in range(blocks):
            inc_copy(b, d).wait_send()
    for side, present in ((0, has_right), (1, has_left)):
        @pl.when(present)
        def _():
            for d in range(subs):
                halo_copy(side, d).wait_send()

    def sent(other):
        r_copy(other).wait_send()
        g_copy(other).wait_send()

    each_far_cell(sent)


def on_device(
    cells, subs,
    direction, neighbours, spacing, scatterer, box_index, translation, response, coarse_map
):
    nrhs, rows, atoms = direction.shape
    nb = neighbours.shape[0]
    terms, _, full = translation.shape
    types = response.shape[0]
    blocks = atoms // BLK
    span, reach, pad = BLK + 2 * WIN, atoms + 2 * WIN, 64
    dma = pltpu.SemaphoreType.DMA
    return pl.pallas_call(
        functools.partial(kernel, cells, subs),
        out_shape=jax.ShapeDtypeStruct(direction.shape, F32),
        in_specs=[pl.BlockSpec(memory_space=pltpu.VMEM)] * 8,
        out_specs=pl.BlockSpec(memory_space=pltpu.VMEM),
        scratch_shapes=[
            pltpu.VMEM((subs, nrhs, rows, reach), F32),
            pltpu.VMEM((nrhs * pad, BOX_DEV), F32),
            pltpu.VMEM((cells, nrhs * pad, BOX_DEV), F32),
            pltpu.VMEM((types * pad, full), F32),
            pltpu.VMEM((cells, types * pad, full), F32),
            pltpu.VMEM((subs, blocks, nrhs * pad, BLK), F32),
            pltpu.VMEM((nb, terms, atoms), F32),
            pltpu.VMEM((nb, atoms), jnp.int32),
            pltpu.VMEM((blocks, terms * span, 2 * BLK), BF16),
            pltpu.VMEM((terms, 2 * nrhs * pad, reach), BF16),
            pltpu.VMEM((terms * pad, full), F32),
            pltpu.VMEM((nrhs, full, reach), F32),
            pltpu.VMEM((nrhs, full, reach), BF16),
            pltpu.VMEM((nrhs, full, reach), BF16),
            pltpu.VMEM((cells, types * pad, full), BF16),
            pltpu.VMEM((cells, types * pad, full), BF16),
            pltpu.VMEM((full, nrhs * BLK), F32),
            dma((subs,)), dma((subs,)), dma((2, subs)), dma((2, subs)),
            dma((cells,)), dma((cells,)), dma((cells,)), dma((cells,)),
            dma((blocks, subs)), dma((blocks, subs)),
        ],
        compiler_params=pltpu.CompilerParams(
            collective_id=0, has_side_effects=True, vmem_limit_bytes=56 * 1024 * 1024
        ),
    )(
        direction, neighbours, spacing, scatterer.reshape(1, atoms), box_index.reshape(1, atoms),
        translation, response, coarse_map,
    )


def solution(mesh):
    in_specs = (
        P("freq", "sub", "cell"),
        P(None, "cell"),
        P(None, "cell"),
        P("cell", None),
        P("cell"),
        P(None, "sub", "freq"),
        P("cell", "sub", "freq"),
        P("sub", "freq"),
    )
    out_specs = P("freq", "sub", "cell")
    return jax.shard_map(
        functools.partial(on_device, mesh.shape["cell"], mesh.shape["sub"]),
        mesh=mesh, in_specs=in_specs, out_specs=out_specs, check_vma=False,
    )
```

```python
import functools

import jax
import jax.numpy as jnp
from jax import lax
from jax.experimental import pallas as pl
from jax.experimental.pallas import tpu as pltpu
from jax.sharding import PartitionSpec as P

BOX_DEV = 16
WIN = 128
BLK = 128
MESH = pl.DeviceIdType.MESH
F32 = jnp.float32
BF16 = jnp.bfloat16
HIGHEST = lax.Precision.HIGHEST


def split(x):
    high = x.astype(BF16)
    return high, (x - high.astype(F32)).astype(BF16)


def dot3(ah, al, bh, bl):
    dot = functools.partial(jnp.dot, preferred_element_type=F32)
    return dot(ah, bh) + (dot(ah, bl) + dot(al, bh))


def kernel(
    cells, subs,
    dir_ref, nbr_ref, spc_ref, kind_ref, box_ref, t_ref, r_ref, cm_ref, out_ref,
    ext, gown, gall, rall, inc, wts, nls, w2, y2, tpad, dfull, dh, dl, rh, rl, ffull,
    dir_send, dir_recv, halo_send, halo_recv, r_send, r_recv, g_send, g_recv, inc_send, inc_recv,
):
    nrhs, rows, atoms = dir_ref.shape
    nb, terms = nbr_ref.shape[0], t_ref.shape[0]
    types, full = r_ref.shape[0], r_ref.shape[2]
    blocks = atoms // BLK
    span = BLK + 2 * WIN
    pad = 64
    cell, sub = lax.axis_index("cell"), lax.axis_index("sub")
    has_left, has_right = cell > 0, cell < cells - 1

    def copy(src, dst, send, recv, to_cell, to_sub):
        return pltpu.make_async_remote_copy(
            src_ref=src, dst_ref=dst, send_sem=send, recv_sem=recv,
            device_id={"cell": to_cell, "sub": to_sub}, device_id_type=MESH,
        )

    def each_far_cell(body):
        def step(other, carry):
            @pl.when(other != cell)
            def _():
                body(other)
            return carry
        lax.fori_loop(0, cells, step, 0)

    barrier = pltpu.get_barrier_semaphore()

    def greet(to_cell, to_sub):
        pl.semaphore_signal(
            barrier, inc=1, device_id={"cell": to_cell, "sub": to_sub}, device_id_type=MESH
        )

    mate, peer = sub + 1 - 2 * lax.rem(sub, 2), lax.rem(sub + 2, subs)
    cross = lax.rem(mate + 2, subs)
    greet(cell, mate)
    greet(cell, peer)
    each_far_cell(lambda other: greet(other, sub))
    pl.semaphore_wait(barrier, cells + 1)

    parts = (pl.ds(0, WIN), pl.ds(WIN, atoms), pl.ds(WIN + atoms, WIN))
    parts_there = ((0, has_left), (2, has_right))

    def rows_copy(part, way, origin, src=None):
        piece = ext.at[origin, :, :, parts[part]]
        to = peer if way == 1 else mate
        return copy(
            piece if src is None else src, piece, dir_send.at[part, way],
            dir_recv.at[part, origin], cell, to,
        )

    def relay(part):
        rows_copy(part, 2, peer).wait_recv()
        rows_copy(part, 2, peer).start()

    def halo_copy(side):
        start = atoms - WIN if side == 0 else 0
        other = cell + 1 if side == 0 else cell - 1
        return copy(
            dir_ref.at[:, :, pl.ds(start, WIN)], ext.at[sub, :, :, parts[2 * side]],
            halo_send.at[side], halo_recv.at[side], other, sub,
        )

    def r_copy(way, shard):
        other = cell + 1 if way == 0 else cell - 1
        piece = rall.at[shard]
        return copy(piece, piece, r_send.at[way, shard], r_recv.at[shard], other, sub)

    def hop(h):
        for way, shard, inside, onward in (
            (0, cell - h, cell - h >= 0, has_right), (1, cell + h, cell + h < cells, has_left)
        ):
            @pl.when(inside)
            def _():
                r_copy(way, shard).wait_recv()

            @pl.when(jnp.logical_and(inside, onward))
            def _():
                r_copy(way, shard).start()

    def g_copy(other):
        return copy(gown, gall.at[cell], g_send.at[other], g_recv.at[cell], other, sub)

    def inc_copy(b, way, origin):
        piece = inc.at[origin, b]
        to = peer if way == 1 else mate
        return copy(piece, piece, inc_send.at[b, way], inc_recv.at[b, origin], cell, to)

    def inc_relay(b):
        inc_copy(b, 2, peer).wait_recv()
        inc_copy(b, 2, peer).start()

    for side, present in ((0, has_right), (1, has_left)):
        @pl.when(present)
        def _():
            halo_copy(side).start()
    for way in (1, 0):
        rows_copy(1, way, sub, dir_ref).start()
    for side, present in ((0, has_left), (1, has_right)):
        @pl.when(jnp.logical_not(present))
        def _():
            place = 0 if side == 0 else WIN + atoms
            ext[:, :, :, pl.ds(place, WIN)] = jnp.zeros((subs, nrhs, rows, WIN), F32)
    ext[sub, :, :, pl.ds(WIN, atoms)] = dir_ref[...]

    rall[cell] = jnp.zeros((types * pad, full), F32)
    for t in range(types):
        rall[cell, t * pad:t * pad + rows, :] = r_ref[t]
    for way, present in ((0, has_right), (1, has_left)):
        @pl.when(present)
        def _():
            r_copy(way, cell).start()

    orders = lax.broadcasted_iota(jnp.int32, (terms, 1), 0).astype(F32)
    wide = nbr_ref[...] - (cell * atoms - WIN)
    near_rows = [wide[n:n + 1] for n in range(nb)]
    plain = []
    for n in range(nb):
        s = spc_ref[n:n + 1, :]
        plain.append(jnp.cos(0.9 * orders * s) / s)
    dead = [None] * nb
    for n in range(nb):
        total = plain[n]
        for m in range(n + 1, nb):
            same = near_rows[n] == near_rows[m]
            total = total + jnp.where(same, plain[m], 0.0)
            flag = same.astype(jnp.int32)
            dead[m] = flag if dead[m] is None else dead[m] | flag
        wts[n] = total
        row = near_rows[n]
        if dead[n] is not None:
            row = jnp.where(dead[n] > 0, -1, row)
        nls[n:n + 1, :] = row

    chunk, group = 32, 8
    for b in range(blocks):
        lanes = slice(b * BLK, (b + 1) * BLK)

        def spread(step, carry):
            base = lax.broadcasted_iota(jnp.int32, (chunk, BLK), 0) + (b * BLK + step * chunk)
            for q0 in range(0, terms, group):
                acc = [jnp.zeros((chunk, BLK), F32)] * group
                for n in range(nb):
                    hit = nls[n:n + 1, lanes] == base
                    for q in range(group):
                        acc[q] = jnp.where(hit, wts[n, q0 + q:q0 + q + 1, lanes], acc[q])
                for q in range(group):
                    high, low = split(acc[q])
                    place = pl.ds(pl.multiple_of((q0 + q) * span + step * chunk, chunk), chunk)
                    w2[b, place, 0:BLK] = high
                    w2[b, place, BLK:2 * BLK] = low
            return carry

        lax.fori_loop(0, span // chunk, spread, 0)
        if b == 0:
            for part, present in parts_there:
                @pl.when(present)
                def _():
                    halo_copy(part // 2).wait_recv()
                    for way in (1, 0):
                        rows_copy(part, way, sub).start()
        if b == blocks // 2:
            relay(1)

    tpad[...] = jnp.zeros_like(tpad)
    for q in range(terms):
        tpad[q * pad:q * pad + rows, :] = t_ref[q]

    for part, present in parts_there:
        @pl.when(present)
        def _():
            relay(part)
    hop(1)
    for origin in (mate, cross):
        rows_copy(1, 0, origin).wait_recv()
    for s in range(subs):
        for k in range(nrhs):
            dfull[k, s * rows:(s + 1) * rows, WIN:WIN + atoms] = ext[s, k, :, WIN:WIN + atoms]

    first_box = cell * BOX_DEV
    box_ids = lax.broadcasted_iota(jnp.int32, (BOX_DEV, 1), 0) + first_box
    member = (box_ref[...] == box_ids).astype(F32)
    member_h = member.astype(BF16)
    gown[...] = jnp.zeros_like(gown)
    nt = (((1,), (1,)), ((), ()))
    for k in range(nrhs):
        ch, cl = split(dfull[k, :, WIN:WIN + atoms])
        dh[k, :, WIN:WIN + atoms] = ch
        dl[k, :, WIN:WIN + atoms] = cl
        sums = lax.dot_general(ch, member_h, nt, preferred_element_type=F32) + lax.dot_general(
            cl, member_h, nt, preferred_element_type=F32
        )
        gown[k * pad:k * pad + rows, :] = jnp.dot(
            cm_ref[...], sums, precision=HIGHEST, preferred_element_type=F32
        )
    each_far_cell(lambda other: g_copy(other).start())
    gall[cell] = gown[...]

    for part, present in parts_there:
        @pl.when(present)
        def _():
            for origin in (mate, cross):
                rows_copy(part, 0, origin).wait_recv()
    for place in (0, WIN + atoms):
        lanes = slice(place, place + WIN)
        for k in range(nrhs):
            for s in range(subs):
                dfull[k, s * rows:(s + 1) * rows, lanes] = ext[s, k, :, lanes]
            high, low = split(dfull[k, :, lanes])
            dh[k, :, lanes] = high
            dl[k, :, lanes] = low

    per = 4
    for q0 in range(0, terms, per):
        th, tl = split(tpad[q0 * pad:(q0 + per) * pad, :])
        for k in range(nrhs):
            high, low = split(dot3(th, tl, dh[k], dl[k]))
            for q in range(per):
                y2[q0 + q, k * pad:(k + 1) * pad, :] = high[q * pad:(q + 1) * pad]
                y2[q0 + q, (nrhs + k) * pad:(nrhs + k + 1) * pad, :] = low[q * pad:(q + 1) * pad]

    if cells > 2:
        hop(2)

    def wait_g(other):
        copy(gown, gall.at[other], g_send.at[other], g_recv.at[other], other, sub).wait_recv()

    each_far_cell(wait_g)
    far_box = jnp.zeros((nrhs * pad, BOX_DEV), F32)
    row_id = lax.broadcasted_iota(jnp.int32, (BOX_DEV, BOX_DEV), 0)
    col_id = lax.broadcasted_iota(jnp.int32, (BOX_DEV, BOX_DEV), 1)
    for c in range(cells):
        offsets = ((row_id + c * BOX_DEV) - (col_id + first_box)).astype(F32)
        green = jnp.where(
            offsets == 0.0, 0.0,
            jnp.cos(1.3 * offsets) / jnp.sqrt(jnp.maximum(jnp.abs(offsets), 1.0)),
        )
        far_box += jnp.dot(gall[c], green, precision=HIGHEST, preferred_element_type=F32)
    fbh, fbl = split(far_box)

    half = nrhs * pad
    for b in range(blocks):
        window = slice(b * BLK, b * BLK + span)
        left = jnp.concatenate([y2[q, :, window] for q in range(terms)], axis=1)
        prod = jnp.dot(left, w2[b], preferred_element_type=F32)
        near = (prod[:half, :BLK] + (prod[:half, BLK:] + prod[half:, :BLK])) + prod[half:, BLK:]
        mb = member_h[:, b * BLK:(b + 1) * BLK]
        far = jnp.dot(fbh, mb, preferred_element_type=F32) + jnp.dot(
            fbl, mb, preferred_element_type=F32
        )
        inc[sub, b] = near + far
        for way in (1, 0):
            inc_copy(b, way, sub).start()
        if b >= 2:
            inc_relay(b - 2)

    def last_hops(h, carry):
        hop(h)
        return carry

    lax.fori_loop(3, cells, last_hops, 0)

    def split_r(c, carry):
        rh[c], rl[c] = split(rall[c])
        return carry

    lax.fori_loop(0, cells, split_r, 0)

    for b in range(blocks):
        lanes = slice(b * BLK, (b + 1) * BLK)
        if b + max(blocks - 2, 0) < blocks:
            inc_relay(b + max(blocks - 2, 0))
        for origin in (mate, cross):
            inc_copy(b, 0, origin).wait_recv()
        for s in range(subs):
            for k in range(nrhs):
                ffull[s * rows:(s + 1) * rows, k * BLK:(k + 1) * BLK] = inc[
                    s, b, k * pad:k * pad + rows, :
                ]
        fh, fl = split(ffull[...])
        kinds = kind_ref[:, lanes]
        kinds = jnp.concatenate([kinds] * nrhs, axis=1)

        def apply(c, total):
            prod = dot3(rh[c], rl[c], fh, fl)
            for t in range(types):
                total = jnp.where(kinds == c * types + t, prod[t * pad:(t + 1) * pad], total)
            return total

        total = jnp.zeros((pad, nrhs * BLK), F32)
        if cells <= 4:
            for c in range(cells):
                total = apply(c, total)
        else:
            total = lax.fori_loop(0, cells, apply, total)
        for k in range(nrhs):
            out_ref[k, :, lanes] = dir_ref[k, :, lanes] - total[:rows, k * BLK:(k + 1) * BLK]

    for way in range(3):
        rows_copy(1, way, sub).wait_send()
        for b in range(blocks):
            inc_copy(b, way, sub).wait_send()
        for part, present in parts_there:
            @pl.when(present)
            def _():
                rows_copy(part, way, sub).wait_send()
    for side, present in ((0, has_right), (1, has_left)):
        @pl.when(present)
        def _():
            halo_copy(side).wait_send()

    def sent(shard, carry):
        for way, goes in (
            (0, jnp.logical_and(shard <= cell, has_right)),
            (1, jnp.logical_and(shard >= cell, has_left)),
        ):
            @pl.when(goes)
            def _():
                r_copy(way, shard).wait_send()
        return carry

    lax.fori_loop(0, cells, sent, 0)
    each_far_cell(lambda other: g_copy(other).wait_send())


def on_device(
    cells, subs,
    direction, neighbours, spacing, scatterer, box_index, translation, response, coarse_map
):
    nrhs, rows, atoms = direction.shape
    nb = neighbours.shape[0]
    terms, _, full = translation.shape
    types = response.shape[0]
    blocks = atoms // BLK
    span, reach, pad = BLK + 2 * WIN, atoms + 2 * WIN, 64
    dma = pltpu.SemaphoreType.DMA
    return pl.pallas_call(
        functools.partial(kernel, cells, subs),
        out_shape=jax.ShapeDtypeStruct(direction.shape, F32),
        in_specs=[pl.BlockSpec(memory_space=pltpu.VMEM)] * 8,
        out_specs=pl.BlockSpec(memory_space=pltpu.VMEM),
        scratch_shapes=[
            pltpu.VMEM((subs, nrhs, rows, reach), F32),
            pltpu.VMEM((nrhs * pad, BOX_DEV), F32),
            pltpu.VMEM((cells, nrhs * pad, BOX_DEV), F32),
            pltpu.VMEM((cells, types * pad, full), F32),
            pltpu.VMEM((subs, blocks, nrhs * pad, BLK), F32),
            pltpu.VMEM((nb, terms, atoms), F32),
            pltpu.VMEM((nb, atoms), jnp.int32),
            pltpu.VMEM((blocks, terms * span, 2 * BLK), BF16),
            pltpu.VMEM((terms, 2 * nrhs * pad, reach), BF16),
            pltpu.VMEM((terms * pad, full), F32),
            pltpu.VMEM((nrhs, full, reach), F32),
            pltpu.VMEM((nrhs, full, reach), BF16),
            pltpu.VMEM((nrhs, full, reach), BF16),
            pltpu.VMEM((cells, types * pad, full), BF16),
            pltpu.VMEM((cells, types * pad, full), BF16),
            pltpu.VMEM((full, nrhs * BLK), F32),
            dma((3, 3)), dma((3, subs)), dma((2,)), dma((2,)),
            dma((2, cells)), dma((cells,)), dma((cells,)), dma((cells,)),
            dma((blocks, 3)), dma((blocks, subs)),
        ],
        compiler_params=pltpu.CompilerParams(
            collective_id=0, has_side_effects=True, vmem_limit_bytes=56 * 1024 * 1024
        ),
    )(
        direction, neighbours, spacing, scatterer.reshape(1, atoms), box_index.reshape(1, atoms),
        translation, response, coarse_map,
    )


def solution(mesh):
    in_specs = (
        P("freq", "sub", "cell"),
        P(None, "cell"),
        P(None, "cell"),
        P("cell", None),
        P("cell"),
        P(None, "sub", "freq"),
        P("cell", "sub", "freq"),
        P("sub", "freq"),
    )
    out_specs = P("freq", "sub", "cell")
    return jax.shard_map(
        functools.partial(on_device, mesh.shape["cell"], mesh.shape["sub"]),
        mesh=mesh, in_specs=in_specs, out_specs=out_specs, check_vma=False,
    )
```

```python
import functools

import jax
import jax.numpy as jnp
from jax import lax
from jax.experimental import pallas as pl
from jax.experimental.pallas import tpu as pltpu
from jax.sharding import PartitionSpec as P

BOX_DEV = 16
WIN = 128
BLK = 128
MESH = pl.DeviceIdType.MESH
F32 = jnp.float32
BF16 = jnp.bfloat16
HIGHEST = lax.Precision.HIGHEST


def split(x):
    high = x.astype(BF16)
    return high, (x - high.astype(F32)).astype(BF16)


def dot3(ah, al, bh, bl):
    dot = functools.partial(jnp.dot, preferred_element_type=F32)
    return dot(ah, bh) + (dot(ah, bl) + dot(al, bh))


def kernel(
    cells, subs,
    raw_ref, nbr_ref, spc_ref, kind_ref, box_ref, t_ref, r_ref, cm_ref, out_ref,
    dir_ref, ext, gown, gall, rall, inc, wts, nls, w2, y2, tpad, dfull, dh, dl, rh, rl, ffull,
    dir_send, dir_recv, halo_send, halo_recv, r_send, r_recv, g_send, g_recv, inc_send, inc_recv,
):
    rows, nrhs, atoms = raw_ref.shape
    nb, terms = nbr_ref.shape[0], t_ref.shape[1]
    types, full = r_ref.shape[1], r_ref.shape[2]
    blocks = atoms // BLK
    span = BLK + 2 * WIN
    pad = 64
    cell, sub = lax.axis_index("cell"), lax.axis_index("sub")
    has_left, has_right = cell > 0, cell < cells - 1

    def copy(src, dst, send, recv, to_cell, to_sub):
        return pltpu.make_async_remote_copy(
            src_ref=src, dst_ref=dst, send_sem=send, recv_sem=recv,
            device_id={"cell": to_cell, "sub": to_sub}, device_id_type=MESH,
        )

    def each_far_cell(body):
        def step(other, carry):
            @pl.when(other != cell)
            def _():
                body(other)
            return carry
        lax.fori_loop(0, cells, step, 0)

    for k in range(nrhs):
        dir_ref[k] = raw_ref[:, k, :]

    barrier = pltpu.get_barrier_semaphore()

    def greet(to_cell, to_sub):
        pl.semaphore_signal(
            barrier, inc=1, device_id={"cell": to_cell, "sub": to_sub}, device_id_type=MESH
        )

    mate, peer = sub + 1 - 2 * lax.rem(sub, 2), lax.rem(sub + 2, subs)
    cross = lax.rem(mate + 2, subs)
    greet(cell, mate)
    greet(cell, peer)
    each_far_cell(lambda other: greet(other, sub))
    pl.semaphore_wait(barrier, cells + 1)

    parts = (pl.ds(0, WIN), pl.ds(WIN, atoms), pl.ds(WIN + atoms, WIN))
    parts_there = ((0, has_left), (2, has_right))

    def rows_copy(part, way, origin, src=None):
        piece = ext.at[origin, :, :, parts[part]]
        to = peer if way == 1 else mate
        return copy(
            piece if src is None else src, piece, dir_send.at[part, way],
            dir_recv.at[part, origin], cell, to,
        )

    def relay(part):
        rows_copy(part, 2, peer).wait_recv()
        rows_copy(part, 2, peer).start()

    def halo_copy(side):
        start = atoms - WIN if side == 0 else 0
        other = cell + 1 if side == 0 else cell - 1
        return copy(
            dir_ref.at[:, :, pl.ds(start, WIN)], ext.at[sub, :, :, parts[2 * side]],
            halo_send.at[side], halo_recv.at[side], other, sub,
        )

    def r_copy(way, shard):
        other = cell + 1 if way == 0 else cell - 1
        piece = rall.at[shard]
        return copy(piece, piece, r_send.at[way, shard], r_recv.at[shard], other, sub)

    def hop(h):
        for way, shard, inside, onward in (
            (0, cell - h, cell - h >= 0, has_right), (1, cell + h, cell + h < cells, has_left)
        ):
            @pl.when(inside)
            def _():
                r_copy(way, shard).wait_recv()

            @pl.when(jnp.logical_and(inside, onward))
            def _():
                r_copy(way, shard).start()

    def g_copy(other):
        return copy(gown, gall.at[cell], g_send.at[other], g_recv.at[cell], other, sub)

    def inc_copy(b, way, origin):
        piece = inc.at[origin, b]
        to = peer if way == 1 else mate
        return copy(piece, piece, inc_send.at[b, way], inc_recv.at[b, origin], cell, to)

    def inc_relay(b):
        inc_copy(b, 2, peer).wait_recv()
        inc_copy(b, 2, peer).start()

    for side, present in ((0, has_right), (1, has_left)):
        @pl.when(present)
        def _():
            halo_copy(side).start()
    for way in (1, 0):
        rows_copy(1, way, sub, dir_ref).start()
    for side, present in ((0, has_left), (1, has_right)):
        @pl.when(jnp.logical_not(present))
        def _():
            place = 0 if side == 0 else WIN + atoms
            ext[:, :, :, pl.ds(place, WIN)] = jnp.zeros((subs, nrhs, rows, WIN), F32)
    ext[sub, :, :, pl.ds(WIN, atoms)] = dir_ref[...]

    rall[cell] = jnp.zeros((types * pad, full), F32)
    for t in range(types):
        rall[cell, t * pad:t * pad + rows, :] = r_ref[:, t, :]
    for way, present in ((0, has_right), (1, has_left)):
        @pl.when(present)
        def _():
            r_copy(way, cell).start()

    orders = lax.broadcasted_iota(jnp.int32, (terms, 1), 0).astype(F32)
    wide = nbr_ref[...] - (cell * atoms - WIN)
    near_rows = [wide[n:n + 1] for n in range(nb)]
    plain = []
    for n in range(nb):
        s = spc_ref[n:n + 1, :]
        plain.append(jnp.cos(0.9 * orders * s) / s)
    dead = [None] * nb
    for n in range(nb):
        total = plain[n]
        for m in range(n + 1, nb):
            same = near_rows[n] == near_rows[m]
            total = total + jnp.where(same, plain[m], 0.0)
            flag = same.astype(jnp.int32)
            dead[m] = flag if dead[m] is None else dead[m] | flag
        wts[n] = total
        row = near_rows[n]
        if dead[n] is not None:
            row = jnp.where(dead[n] > 0, -1, row)
        nls[n:n + 1, :] = row

    chunk, group = 32, 8
    for b in range(blocks):
        lanes = slice(b * BLK, (b + 1) * BLK)

        def spread(step, carry):
            base = lax.broadcasted_iota(jnp.int32, (chunk, BLK), 0) + (b * BLK + step * chunk)
            for q0 in range(0, terms, group):
                acc = [jnp.zeros((chunk, BLK), F32)] * group
                for n in range(nb):
                    hit = nls[n:n + 1, lanes] == base
                    for q in range(group):
                        acc[q] = jnp.where(hit, wts[n, q0 + q:q0 + q + 1, lanes], acc[q])
                for q in range(group):
                    high, low = split(acc[q])
                    place = pl.ds(pl.multiple_of((q0 + q) * span + step * chunk, chunk), chunk)
                    w2[b, place, 0:BLK] = high
                    w2[b, place, BLK:2 * BLK] = low
            return carry

        lax.fori_loop(0, span // chunk, spread, 0)
        if b == 0:
            for part, present in parts_there:
                @pl.when(present)
                def _():
                    halo_copy(part // 2).wait_recv()
                    for way in (1, 0):
                        rows_copy(part, way, sub).start()
        if b == blocks // 2:
            relay(1)

    hop(1)
    tpad[...] = jnp.zeros_like(tpad)
    for q in range(terms):
        tpad[q * pad:q * pad + rows, :] = t_ref[:, q, :]

    for part, present in parts_there:
        @pl.when(present)
        def _():
            relay(part)
    for origin in (mate, cross):
        rows_copy(1, 0, origin).wait_recv()
    for s in range(subs):
        for k in range(nrhs):
            dfull[k, s * rows:(s + 1) * rows, WIN:WIN + atoms] = ext[s, k, :, WIN:WIN + atoms]

    first_box = cell * BOX_DEV
    box_ids = lax.broadcasted_iota(jnp.int32, (BOX_DEV, 1), 0) + first_box
    member = (box_ref[...] == box_ids).astype(F32)
    member_h = member.astype(BF16)
    gown[...] = jnp.zeros_like(gown)
    nt = (((1,), (1,)), ((), ()))
    for k in range(nrhs):
        ch, cl = split(dfull[k, :, WIN:WIN + atoms])
        dh[k, :, WIN:WIN + atoms] = ch
        dl[k, :, WIN:WIN + atoms] = cl
        sums = lax.dot_general(ch, member_h, nt, preferred_element_type=F32) + lax.dot_general(
            cl, member_h, nt, preferred_element_type=F32
        )
        gown[k * pad:k * pad + rows, :] = jnp.dot(
            cm_ref[...], sums, precision=HIGHEST, preferred_element_type=F32
        )
    each_far_cell(lambda other: g_copy(other).start())
    gall[cell] = gown[...]

    for part, present in parts_there:
        @pl.when(present)
        def _():
            for origin in (mate, cross):
                rows_copy(part, 0, origin).wait_recv()
    for place in (0, WIN + atoms):
        lanes = slice(place, place + WIN)
        for k in range(nrhs):
            for s in range(subs):
                dfull[k, s * rows:(s + 1) * rows, lanes] = ext[s, k, :, lanes]
            high, low = split(dfull[k, :, lanes])
            dh[k, :, lanes] = high
            dl[k, :, lanes] = low

    if cells > 2:
        hop(2)

    per = 4
    for q0 in range(0, terms, per):
        th, tl = split(tpad[q0 * pad:(q0 + per) * pad, :])
        for k in range(nrhs):
            high, low = split(dot3(th, tl, dh[k], dl[k]))
            for q in range(per):
                y2[q0 + q, k * pad:(k + 1) * pad, :] = high[q * pad:(q + 1) * pad]
                y2[q0 + q, (nrhs + k) * pad:(nrhs + k + 1) * pad, :] = low[q * pad:(q + 1) * pad]

    def wait_g(other):
        copy(gown, gall.at[other], g_send.at[other], g_recv.at[other], other, sub).wait_recv()

    each_far_cell(wait_g)
    far_box = jnp.zeros((nrhs * pad, BOX_DEV), F32)
    row_id = lax.broadcasted_iota(jnp.int32, (BOX_DEV, BOX_DEV), 0)
    col_id = lax.broadcasted_iota(jnp.int32, (BOX_DEV, BOX_DEV), 1)
    for c in range(cells):
        offsets = ((row_id + c * BOX_DEV) - (col_id + first_box)).astype(F32)
        green = jnp.where(
            offsets == 0.0, 0.0,
            jnp.cos(1.3 * offsets) / jnp.sqrt(jnp.maximum(jnp.abs(offsets), 1.0)),
        )
        far_box += jnp.dot(gall[c], green, precision=HIGHEST, preferred_element_type=F32)
    fbh, fbl = split(far_box)

    half = nrhs * pad
    for b in range(blocks):
        window = slice(b * BLK, b * BLK + span)
        left = jnp.concatenate([y2[q, :, window] for q in range(terms)], axis=1)
        prod = jnp.dot(left, w2[b], preferred_element_type=F32)
        near = (prod[:half, :BLK] + (prod[:half, BLK:] + prod[half:, :BLK])) + prod[half:, BLK:]
        mb = member_h[:, b * BLK:(b + 1) * BLK]
        far = jnp.dot(fbh, mb, preferred_element_type=F32) + jnp.dot(
            fbl, mb, preferred_element_type=F32
        )
        inc[sub, b] = near + far
        for way in (1, 0):
            inc_copy(b, way, sub).start()
        if b >= 2:
            inc_relay(b - 2)

    def last_hops(h, carry):
        hop(h)
        return carry

    lax.fori_loop(3, cells, last_hops, 0)

    def split_r(c, carry):
        rh[c], rl[c] = split(rall[c])
        return carry

    lax.fori_loop(0, cells, split_r, 0)

    for b in range(blocks):
        lanes = slice(b * BLK, (b + 1) * BLK)
        if b + max(blocks - 2, 0) < blocks:
            inc_relay(b + max(blocks - 2, 0))
        for origin in (mate, cross):
            inc_copy(b, 0, origin).wait_recv()
        for s in range(subs):
            for k in range(nrhs):
                ffull[s * rows:(s + 1) * rows, k * BLK:(k + 1) * BLK] = inc[
                    s, b, k * pad:k * pad + rows, :
                ]
        fh, fl = split(ffull[...])
        kinds = kind_ref[:, lanes]
        kinds = jnp.concatenate([kinds] * nrhs, axis=1)

        def apply(c, total):
            prod = dot3(rh[c], rl[c], fh, fl)
            for t in range(types):
                total = jnp.where(kinds == c * types + t, prod[t * pad:(t + 1) * pad], total)
            return total

        total = jnp.zeros((pad, nrhs * BLK), F32)
        if cells <= 4:
            for c in range(cells):
                total = apply(c, total)
        else:
            total = lax.fori_loop(0, cells, apply, total)
        for k in range(nrhs):
            out_ref[:, k, lanes] = dir_ref[k, :, lanes] - total[:rows, k * BLK:(k + 1) * BLK]

    for way in range(3):
        rows_copy(1, way, sub).wait_send()
        for b in range(blocks):
            inc_copy(b, way, sub).wait_send()
        for part, present in parts_there:
            @pl.when(present)
            def _():
                rows_copy(part, way, sub).wait_send()
    for side, present in ((0, has_right), (1, has_left)):
        @pl.when(present)
        def _():
            halo_copy(side).wait_send()

    def sent(shard, carry):
        for way, goes in (
            (0, jnp.logical_and(shard <= cell, has_right)),
            (1, jnp.logical_and(shard >= cell, has_left)),
        ):
            @pl.when(goes)
            def _():
                r_copy(way, shard).wait_send()
        return carry

    lax.fori_loop(0, cells, sent, 0)
    each_far_cell(lambda other: g_copy(other).wait_send())


def on_device(
    cells, subs,
    direction, neighbours, spacing, scatterer, box_index, translation, response, coarse_map
):
    nrhs, rows, atoms = direction.shape
    nb = neighbours.shape[0]
    terms, _, full = translation.shape
    types = response.shape[0]
    blocks = atoms // BLK
    span, reach, pad = BLK + 2 * WIN, atoms + 2 * WIN, 64
    dma = pltpu.SemaphoreType.DMA
    product = pl.pallas_call(
        functools.partial(kernel, cells, subs),
        out_shape=jax.ShapeDtypeStruct((rows, nrhs, atoms), F32),
        in_specs=[pl.BlockSpec(memory_space=pltpu.VMEM)] * 8,
        out_specs=pl.BlockSpec(memory_space=pltpu.VMEM),
        scratch_shapes=[
            pltpu.VMEM((nrhs, rows, atoms), F32),
            pltpu.VMEM((subs, nrhs, rows, reach), F32),
            pltpu.VMEM((nrhs * pad, BOX_DEV), F32),
            pltpu.VMEM((cells, nrhs * pad, BOX_DEV), F32),
            pltpu.VMEM((cells, types * pad, full), F32),
            pltpu.VMEM((subs, blocks, nrhs * pad, BLK), F32),
            pltpu.VMEM((nb, terms, atoms), F32),
            pltpu.VMEM((nb, atoms), jnp.int32),
            pltpu.VMEM((blocks, terms * span, 2 * BLK), BF16),
            pltpu.VMEM((terms, 2 * nrhs * pad, reach), BF16),
            pltpu.VMEM((terms * pad, full), F32),
            pltpu.VMEM((nrhs, full, reach), F32),
            pltpu.VMEM((nrhs, full, reach), BF16),
            pltpu.VMEM((nrhs, full, reach), BF16),
            pltpu.VMEM((cells, types * pad, full), BF16),
            pltpu.VMEM((cells, types * pad, full), BF16),
            pltpu.VMEM((full, nrhs * BLK), F32),
            dma((3, 3)), dma((3, subs)), dma((2,)), dma((2,)),
            dma((2, cells)), dma((cells,)), dma((cells,)), dma((cells,)),
            dma((blocks, 3)), dma((blocks, subs)),
        ],
        compiler_params=pltpu.CompilerParams(
            collective_id=0, has_side_effects=True, vmem_limit_bytes=56 * 1024 * 1024
        ),
    )(
        jnp.transpose(direction, (1, 0, 2)), neighbours, spacing, scatterer.reshape(1, atoms), box_index.reshape(1, atoms),
        jnp.transpose(translation, (1, 0, 2)), jnp.transpose(response, (1, 0, 2)), coarse_map,
    )
    return jnp.transpose(product, (1, 0, 2))


def solution(mesh):
    in_specs = (
        P("freq", "sub", "cell"),
        P(None, "cell"),
        P(None, "cell"),
        P("cell", None),
        P("cell"),
        P(None, "sub", "freq"),
        P("cell", "sub", "freq"),
        P("sub", "freq"),
    )
    out_specs = P("freq", "sub", "cell")
    return jax.shard_map(
        functools.partial(on_device, mesh.shape["cell"], mesh.shape["sub"]),
        mesh=mesh, in_specs=in_specs, out_specs=out_specs, check_vma=False,
    )
```

```python
import functools

import jax
import jax.numpy as jnp
from jax import lax
from jax.experimental import pallas as pl
from jax.experimental.pallas import tpu as pltpu
from jax.sharding import PartitionSpec as P

BOX_DEV = 16
WIN = 128
BLK = 128
MESH = pl.DeviceIdType.MESH
F32 = jnp.float32
BF16 = jnp.bfloat16
HIGHEST = lax.Precision.HIGHEST


def split(x):
    high = x.astype(BF16)
    return high, (x - high.astype(F32)).astype(BF16)


def dot3(ah, al, bh, bl):
    dot = functools.partial(jnp.dot, preferred_element_type=F32)
    return dot(ah, bh) + (dot(ah, bl) + dot(al, bh))


def kernel(
    cells, subs,
    raw_ref, nbr_ref, spc_ref, kind_ref, box_ref, t_ref, r_ref, cm_ref, out_ref,
    dir_ref, ext, gown, gall, rall, inc, wts, nls, w2, y2, tpad, dfull, dh, dl, rh, rl, ffull,
    dir_send, dir_recv, halo_send, halo_recv, r_send, r_recv, g_send, g_recv, inc_send, inc_recv,
):
    rows, nrhs, atoms = raw_ref.shape
    nb, terms = nbr_ref.shape[0], t_ref.shape[1]
    types, full = r_ref.shape[1], r_ref.shape[2]
    blocks = atoms // BLK
    span = BLK + 2 * WIN
    pad = 64
    cell, sub = lax.axis_index("cell"), lax.axis_index("sub")
    has_left, has_right = cell > 0, cell < cells - 1

    def copy(src, dst, send, recv, to_cell, to_sub):
        return pltpu.make_async_remote_copy(
            src_ref=src, dst_ref=dst, send_sem=send, recv_sem=recv,
            device_id={"cell": to_cell, "sub": to_sub}, device_id_type=MESH,
        )

    def each_far_cell(body):
        def step(other, carry):
            @pl.when(other != cell)
            def _():
                body(other)
            return carry
        lax.fori_loop(0, cells, step, 0)

    for k in range(nrhs):
        dir_ref[k] = raw_ref[:, k, :]

    barrier = pltpu.get_barrier_semaphore()

    def greet(to_cell, to_sub):
        pl.semaphore_signal(
            barrier, inc=1, device_id={"cell": to_cell, "sub": to_sub}, device_id_type=MESH
        )

    mate, peer = sub + 1 - 2 * lax.rem(sub, 2), lax.rem(sub + 2, subs)
    cross = lax.rem(mate + 2, subs)
    greet(cell, mate)
    greet(cell, peer)
    each_far_cell(lambda other: greet(other, sub))
    pl.semaphore_wait(barrier, cells + 1)

    parts = (pl.ds(0, WIN), pl.ds(WIN, atoms), pl.ds(WIN + atoms, WIN))
    parts_there = ((0, has_left), (2, has_right))

    def rows_copy(part, way, origin, src=None):
        piece = ext.at[origin, :, :, parts[part]]
        to = peer if way == 1 else mate
        return copy(
            piece if src is None else src, piece, dir_send.at[part, way],
            dir_recv.at[part, origin], cell, to,
        )

    def relay(part):
        rows_copy(part, 2, peer).wait_recv()
        rows_copy(part, 2, peer).start()

    def halo_copy(side):
        start = atoms - WIN if side == 0 else 0
        other = cell + 1 if side == 0 else cell - 1
        return copy(
            dir_ref.at[:, :, pl.ds(start, WIN)], ext.at[sub, :, :, parts[2 * side]],
            halo_send.at[side], halo_recv.at[side], other, sub,
        )

    def r_copy(way, shard):
        other = cell + 1 if way == 0 else cell - 1
        piece = rall.at[shard]
        return copy(piece, piece, r_send.at[way, shard], r_recv.at[shard], other, sub)

    def hop(h):
        for way, shard, inside, onward in (
            (0, cell - h, cell - h >= 0, has_right), (1, cell + h, cell + h < cells, has_left)
        ):
            @pl.when(inside)
            def _():
                r_copy(way, shard).wait_recv()

            @pl.when(jnp.logical_and(inside, onward))
            def _():
                r_copy(way, shard).start()

    def g_copy(other):
        return copy(gown, gall.at[cell], g_send.at[other], g_recv.at[cell], other, sub)

    def inc_copy(b, way, origin):
        piece = inc.at[origin, b]
        to = peer if way == 1 else mate
        return copy(piece, piece, inc_send.at[b, way], inc_recv.at[b, origin], cell, to)

    def inc_relay(b):
        inc_copy(b, 2, peer).wait_recv()
        inc_copy(b, 2, peer).start()

    for side, present in ((0, has_right), (1, has_left)):
        @pl.when(present)
        def _():
            halo_copy(side).start()
    for way in (1, 0):
        rows_copy(1, way, sub, dir_ref).start()
    for side, present in ((0, has_left), (1, has_right)):
        @pl.when(jnp.logical_not(present))
        def _():
            place = 0 if side == 0 else WIN + atoms
            ext[:, :, :, pl.ds(place, WIN)] = jnp.zeros((subs, nrhs, rows, WIN), F32)
    ext[sub, :, :, pl.ds(WIN, atoms)] = dir_ref[...]

    rall[cell] = jnp.zeros((types * pad, full), F32)
    for t in range(types):
        rall[cell, t * pad:t * pad + rows, :] = r_ref[:, t, :]
    for way, present in ((0, has_right), (1, has_left)):
        @pl.when(present)
        def _():
            r_copy(way, cell).start()

    orders = lax.broadcasted_iota(jnp.int32, (terms, 1), 0).astype(F32)
    wide = nbr_ref[...] - (cell * atoms - WIN)
    near_rows = [wide[n:n + 1] for n in range(nb)]
    plain = []
    for n in range(nb):
        s = spc_ref[n:n + 1, :]
        plain.append(jnp.cos(0.9 * orders * s) / s)
    dead = [None] * nb
    for n in range(nb):
        total = plain[n]
        for m in range(n + 1, nb):
            same = near_rows[n] == near_rows[m]
            total = total + jnp.where(same, plain[m], 0.0)
            flag = same.astype(jnp.int32)
            dead[m] = flag if dead[m] is None else dead[m] | flag
        wts[n] = total
        row = near_rows[n]
        if dead[n] is not None:
            row = jnp.where(dead[n] > 0, -1, row)
        nls[n:n + 1, :] = row

    chunk, group = 32, 8
    for b in range(blocks):
        lanes = slice(b * BLK, (b + 1) * BLK)

        def spread(step, carry):
            base = lax.broadcasted_iota(jnp.int32, (chunk, BLK), 0) + (b * BLK + step * chunk)
            for q0 in range(0, terms, group):
                acc = [jnp.zeros((chunk, BLK), F32)] * group
                for n in range(nb):
                    hit = nls[n:n + 1, lanes] == base
                    for q in range(group):
                        acc[q] = jnp.where(hit, wts[n, q0 + q:q0 + q + 1, lanes], acc[q])
                for q in range(group):
                    high, low = split(acc[q])
                    place = pl.ds(pl.multiple_of((q0 + q) * span + step * chunk, chunk), chunk)
                    w2[b, place, 0:BLK] = high
                    w2[b, place, BLK:2 * BLK] = low
            return carry

        lax.fori_loop(0, span // chunk, spread, 0)
        if b == 0:
            for part, present in parts_there:
                @pl.when(present)
                def _():
                    halo_copy(part // 2).wait_recv()
                    for way in (1, 0):
                        rows_copy(part, way, sub).start()
        if b == blocks // 2:
            relay(1)

    for part, present in parts_there:
        @pl.when(present)
        def _():
            relay(part)
    hop(1)
    tpad[...] = jnp.zeros_like(tpad)
    for q in range(terms):
        tpad[q * pad:q * pad + rows, :] = t_ref[:, q, :]

    for origin in (mate, cross):
        rows_copy(1, 0, origin).wait_recv()
    for s in range(subs):
        for k in range(nrhs):
            dfull[k, s * rows:(s + 1) * rows, WIN:WIN + atoms] = ext[s, k, :, WIN:WIN + atoms]

    first_box = cell * BOX_DEV
    box_ids = lax.broadcasted_iota(jnp.int32, (BOX_DEV, 1), 0) + first_box
    member = (box_ref[...] == box_ids).astype(F32)
    member_h = member.astype(BF16)
    gown[...] = jnp.zeros_like(gown)
    nt = (((1,), (1,)), ((), ()))
    for k in range(nrhs):
        ch, cl = split(dfull[k, :, WIN:WIN + atoms])
        dh[k, :, WIN:WIN + atoms] = ch
        dl[k, :, WIN:WIN + atoms] = cl
        sums = lax.dot_general(ch, member_h, nt, preferred_element_type=F32) + lax.dot_general(
            cl, member_h, nt, preferred_element_type=F32
        )
        gown[k * pad:k * pad + rows, :] = jnp.dot(
            cm_ref[...], sums, precision=HIGHEST, preferred_element_type=F32
        )
    each_far_cell(lambda other: g_copy(other).start())
    gall[cell] = gown[...]

    per = 4

    def translate(lanes):
        for q0 in range(0, terms, per):
            th, tl = split(tpad[q0 * pad:(q0 + per) * pad, :])
            for k in range(nrhs):
                right = [jnp.concatenate([d[k, :, part] for part in lanes], axis=1) for d in (dh, dl)]
                high, low = split(dot3(th, tl, *right))
                at = 0
                for part in lanes:
                    here = slice(at, at + part.stop - part.start)
                    at = here.stop
                    for q in range(per):
                        own = slice(q * pad, (q + 1) * pad)
                        y2[q0 + q, k * pad:(k + 1) * pad, part] = high[own, here]
                        y2[q0 + q, (nrhs + k) * pad:(nrhs + k + 1) * pad, part] = low[own, here]

    translate([slice(WIN, WIN + atoms)])
    if cells > 2:
        hop(2)

    for part, present in parts_there:
        @pl.when(present)
        def _():
            for origin in (mate, cross):
                rows_copy(part, 0, origin).wait_recv()
    for place in (0, WIN + atoms):
        lanes = slice(place, place + WIN)
        for k in range(nrhs):
            for s in range(subs):
                dfull[k, s * rows:(s + 1) * rows, lanes] = ext[s, k, :, lanes]
            high, low = split(dfull[k, :, lanes])
            dh[k, :, lanes] = high
            dl[k, :, lanes] = low

    translate([slice(0, WIN), slice(WIN + atoms, atoms + 2 * WIN)])

    def wait_g(other):
        copy(gown, gall.at[other], g_send.at[other], g_recv.at[other], other, sub).wait_recv()

    each_far_cell(wait_g)
    far_box = jnp.zeros((nrhs * pad, BOX_DEV), F32)
    row_id = lax.broadcasted_iota(jnp.int32, (BOX_DEV, BOX_DEV), 0)
    col_id = lax.broadcasted_iota(jnp.int32, (BOX_DEV, BOX_DEV), 1)
    for c in range(cells):
        offsets = ((row_id + c * BOX_DEV) - (col_id + first_box)).astype(F32)
        green = jnp.where(
            offsets == 0.0, 0.0,
            jnp.cos(1.3 * offsets) / jnp.sqrt(jnp.maximum(jnp.abs(offsets), 1.0)),
        )
        far_box += jnp.dot(gall[c], green, precision=HIGHEST, preferred_element_type=F32)
    fbh, fbl = split(far_box)

    half = nrhs * pad
    for b in range(blocks):
        window = slice(b * BLK, b * BLK + span)
        left = jnp.concatenate([y2[q, :, window] for q in range(terms)], axis=1)
        prod = jnp.dot(left, w2[b], preferred_element_type=F32)
        near = (prod[:half, :BLK] + (prod[:half, BLK:] + prod[half:, :BLK])) + prod[half:, BLK:]
        mb = member_h[:, b * BLK:(b + 1) * BLK]
        far = jnp.dot(fbh, mb, preferred_element_type=F32) + jnp.dot(
            fbl, mb, preferred_element_type=F32
        )
        inc[sub, b] = near + far
        for way in (1, 0):
            inc_copy(b, way, sub).start()
        if b >= 2:
            inc_relay(b - 2)

    def last_hops(h, carry):
        hop(h)
        return carry

    lax.fori_loop(3, cells, last_hops, 0)

    def split_r(c, carry):
        rh[c], rl[c] = split(rall[c])
        return carry

    lax.fori_loop(0, cells, split_r, 0)

    for b in range(blocks):
        lanes = slice(b * BLK, (b + 1) * BLK)
        if b + max(blocks - 2, 0) < blocks:
            inc_relay(b + max(blocks - 2, 0))
        for origin in (mate, cross):
            inc_copy(b, 0, origin).wait_recv()
        for s in range(subs):
            for k in range(nrhs):
                ffull[s * rows:(s + 1) * rows, k * BLK:(k + 1) * BLK] = inc[
                    s, b, k * pad:k * pad + rows, :
                ]
        fh, fl = split(ffull[...])
        kinds = kind_ref[:, lanes]
        kinds = jnp.concatenate([kinds] * nrhs, axis=1)

        def apply(c, total):
            prod = dot3(rh[c], rl[c], fh, fl)
            for t in range(types):
                total = jnp.where(kinds == c * types + t, prod[t * pad:(t + 1) * pad], total)
            return total

        total = jnp.zeros((pad, nrhs * BLK), F32)
        if cells <= 4:
            for c in range(cells):
                total = apply(c, total)
        else:
            total = lax.fori_loop(0, cells, apply, total)
        for k in range(nrhs):
            out_ref[:, k, lanes] = dir_ref[k, :, lanes] - total[:rows, k * BLK:(k + 1) * BLK]

    for way in range(3):
        rows_copy(1, way, sub).wait_send()
        for b in range(blocks):
            inc_copy(b, way, sub).wait_send()
        for part, present in parts_there:
            @pl.when(present)
            def _():
                rows_copy(part, way, sub).wait_send()
    for side, present in ((0, has_right), (1, has_left)):
        @pl.when(present)
        def _():
            halo_copy(side).wait_send()

    def sent(shard, carry):
        for way, goes in (
            (0, jnp.logical_and(shard <= cell, has_right)),
            (1, jnp.logical_and(shard >= cell, has_left)),
        ):
            @pl.when(goes)
            def _():
                r_copy(way, shard).wait_send()
        return carry

    lax.fori_loop(0, cells, sent, 0)
    each_far_cell(lambda other: g_copy(other).wait_send())


def on_device(
    cells, subs,
    direction, neighbours, spacing, scatterer, box_index, translation, response, coarse_map
):
    nrhs, rows, atoms = direction.shape
    nb = neighbours.shape[0]
    terms, _, full = translation.shape
    types = response.shape[0]
    blocks = atoms // BLK
    span, reach, pad = BLK + 2 * WIN, atoms + 2 * WIN, 64
    dma = pltpu.SemaphoreType.DMA
    product = pl.pallas_call(
        functools.partial(kernel, cells, subs),
        out_shape=jax.ShapeDtypeStruct((rows, nrhs, atoms), F32),
        in_specs=[pl.BlockSpec(memory_space=pltpu.VMEM)] * 8,
        out_specs=pl.BlockSpec(memory_space=pltpu.VMEM),
        scratch_shapes=[
            pltpu.VMEM((nrhs, rows, atoms), F32),
            pltpu.VMEM((subs, nrhs, rows, reach), F32),
            pltpu.VMEM((nrhs * pad, BOX_DEV), F32),
            pltpu.VMEM((cells, nrhs * pad, BOX_DEV), F32),
            pltpu.VMEM((cells, types * pad, full), F32),
            pltpu.VMEM((subs, blocks, nrhs * pad, BLK), F32),
            pltpu.VMEM((nb, terms, atoms), F32),
            pltpu.VMEM((nb, atoms), jnp.int32),
            pltpu.VMEM((blocks, terms * span, 2 * BLK), BF16),
            pltpu.VMEM((terms, 2 * nrhs * pad, reach), BF16),
            pltpu.VMEM((terms * pad, full), F32),
            pltpu.VMEM((nrhs, full, reach), F32),
            pltpu.VMEM((nrhs, full, reach), BF16),
            pltpu.VMEM((nrhs, full, reach), BF16),
            pltpu.VMEM((cells, types * pad, full), BF16),
            pltpu.VMEM((cells, types * pad, full), BF16),
            pltpu.VMEM((full, nrhs * BLK), F32),
            dma((3, 3)), dma((3, subs)), dma((2,)), dma((2,)),
            dma((2, cells)), dma((cells,)), dma((cells,)), dma((cells,)),
            dma((blocks, 3)), dma((blocks, subs)),
        ],
        compiler_params=pltpu.CompilerParams(
            collective_id=0, has_side_effects=True, vmem_limit_bytes=56 * 1024 * 1024
        ),
    )(
        jnp.transpose(direction, (1, 0, 2)), neighbours, spacing, scatterer.reshape(1, atoms), box_index.reshape(1, atoms),
        jnp.transpose(translation, (1, 0, 2)), jnp.transpose(response, (1, 0, 2)), coarse_map,
    )
    return jnp.transpose(product, (1, 0, 2))


def solution(mesh):
    in_specs = (
        P("freq", "sub", "cell"),
        P(None, "cell"),
        P(None, "cell"),
        P("cell", None),
        P("cell"),
        P(None, "sub", "freq"),
        P("cell", "sub", "freq"),
        P("sub", "freq"),
    )
    out_specs = P("freq", "sub", "cell")
    return jax.shard_map(
        functools.partial(on_device, mesh.shape["cell"], mesh.shape["sub"]),
        mesh=mesh, in_specs=in_specs, out_specs=out_specs, check_vma=False,
    )
```
